256 devices in a mesh: group: 16 (over y, x), ingroup: 16 (over z, core).
Axes of the slice: x: 4, y: 4, z: 8, core: 2. Of those that a mesh axis runs over, the one named last changes fastest.
Arguments:
- activations: bfloat16 [16384, 3584], P(('group', 'ingroup')), may hold values from -6 to 6
- gate_weights: bfloat16 [256, 1792, 1024], P(('group', 'ingroup')), may hold values from -0.09375 to 0.09375
- up_weights: bfloat16 [256, 1792, 1024], P(('group', 'ingroup')), may hold values from -0.09375 to 0.09375
- down_weights: bfloat16 [256, 1024, 1792], P(('group', 'ingroup')), may hold values from -0.375 to 0.375
- expert_ids: int32 [16384, 8], P(('group', 'ingroup')), may hold values from 0 to 127, as said below
- gate_scores: int32 [16384, 8], P(('group', 'ingroup')), may hold values from 1 to 15
- arrival_pos: int32 [16384], P(('group', 'ingroup')), may hold values from 0 to 63, as said below
Outputs:
- expert_mix: bfloat16 [16384, 3584], P(('group', 'ingroup'))
The draws below stay inside these ranges and needn't reach their ends.
Inputs may be any that keep to these rules, and one draw needn't show every extreme that they name: `expert_ids`: each row names 8 different experts, two from each of 4 different groups. Among one device's 64 rows no expert is named more than 6 times and no group by more than 24 rows; on every device some expert is named exactly 6 times and some group by exactly 24 rows. `arrival_pos`: within each device's 64 rows the values are a permutation.
All inputs are finite; a program needn't handle non-finite values.
Results may differ from the reference program's by a relative error of at most 0.0077.
Values may be sent and summed in bfloat16 or wider, within the bound.
No kernel may reach another device: no remote copies, remote signals or barrier semaphores. Data moves between devices by JAX's collectives and lax.ppermute only.
A program may use at most 128 MiB of HBM per device.

```python
import jax
import jax.numpy as jnp
from jax import lax

D = 3584
H = 1024
TOPK = 8
TOPG = 4
TOK_DEV = 64
EXP_GROUP = 8
EXPERTS = 128
TOKENS = 16384
HOT_GROUPS = 4
GROUP_MOST = 24
CAP = 1024


def routing_draw(key):
    group_count = EXPERTS // EXP_GROUP
    block_count = TOKENS // TOK_DEV
    base_key = jax.random.fold_in(key, 101)
    global_order = jax.random.permutation(jax.random.fold_in(base_key, 7), group_count)
    remaining = TOPG * TOK_DEV - HOT_GROUPS * GROUP_MOST
    cold_count = group_count - HOT_GROUPS
    cold_room = cold_count * GROUP_MOST - remaining
    cut_rows = 0
    if HOT_GROUPS >= 2:
        cut_rows = min(GROUP_MOST - 2 * GROUP_MOST // 3, cold_room)
    cut_place = jax.random.randint(jax.random.fold_in(base_key, 13), (), 0, HOT_GROUPS)
    order_index = jnp.arange(group_count, dtype=jnp.int32)

    def sizes_for(moved):
        spread_rows = remaining + moved
        cold_base = spread_rows // cold_count
        cold_extra = spread_rows % cold_count
        by_place = jnp.where(order_index < HOT_GROUPS, GROUP_MOST, cold_base + (order_index - HOT_GROUPS < cold_extra).astype(jnp.int32))
        by_place = by_place - moved * (order_index == cut_place).astype(jnp.int32)
        return jnp.zeros((group_count,), jnp.int32).at[global_order].set(by_place.astype(jnp.int32))
    drawn_sizes = sizes_for(0)
    reduced_sizes = sizes_for(cut_rows)
    cut_blocks = jax.random.randint(jax.random.fold_in(base_key, 9), (), block_count // 8, block_count // 2 + 1)
    block_rank = jax.random.permutation(jax.random.fold_in(base_key, 11), block_count)
    block_cut = block_rank < cut_blocks

    def one_block(block_key, is_cut):
        group_sizes = jnp.where(is_cut, reduced_sizes, drawn_sizes)
        first_key, second_key, third_key = jax.random.split(block_key, 3)
        block_order = jax.random.permutation(first_key, group_count)
        sizes_here = group_sizes[block_order]
        run_ends = jnp.cumsum(sizes_here).astype(jnp.int32)
        run_starts = run_ends - sizes_here
        unit_index = jnp.arange(TOPG * TOK_DEV, dtype=jnp.int32)
        run_index = jnp.sum((unit_index[:, None] >= run_ends[None, :]).astype(jnp.int32), axis=1)
        unit_group = block_order[run_index]
        within_run = unit_index - run_starts[run_index]
        member_orders = jax.vmap(lambda member_key: jax.random.permutation(member_key, EXP_GROUP))(jax.random.split(second_key, group_count))
        first_member = member_orders[unit_group, 2 * within_run % EXP_GROUP]
        second_member = member_orders[unit_group, (2 * within_run + 1) % EXP_GROUP]
        token_place = unit_index % TOK_DEV
        round_index = unit_index // TOK_DEV
        picks_table = jnp.zeros((TOK_DEV, TOPK), jnp.int32)
        picks_table = picks_table.at[token_place, 2 * round_index].set(unit_group * EXP_GROUP + first_member)
        picks_table = picks_table.at[token_place, 2 * round_index + 1].set(unit_group * EXP_GROUP + second_member)
        token_order = jax.random.permutation(third_key, TOK_DEV)
        return picks_table[token_order]
    block_keys = jax.random.split(base_key, block_count)
    picks = jax.vmap(one_block)(block_keys, block_cut).reshape(TOKENS, TOPK).astype(jnp.int32)
    return (picks, global_order[:HOT_GROUPS].astype(jnp.int32))


def draw_expert_ids(key, part):
    picks, hot_list = routing_draw(key)
    return picks


def draw_arrival_pos(key, part):
    picks, hot_list = routing_draw(key)
    key = jax.random.fold_in(key, 202)
    block_count = TOKENS // TOK_DEV
    early_pick = jax.random.randint(jax.random.fold_in(key, 1), (block_count,), 0, HOT_GROUPS)
    early_group = hot_list[early_pick]
    picked_groups = picks.reshape(block_count, TOK_DEV, TOPK) // EXP_GROUP
    picks_early = jnp.any(picked_groups == early_group[:, None, None], axis=2).astype(jnp.int32)
    tie_break = jax.vmap(lambda block_key: jax.random.permutation(block_key, TOK_DEV))(jax.random.split(jax.random.fold_in(key, 2), block_count))
    priority = (1 - picks_early) * TOK_DEV + tie_break.astype(jnp.int32)
    arrival_order = jnp.argsort(priority, axis=1, stable=True)
    positions = jnp.argsort(arrival_order, axis=1, stable=True)
    return positions.reshape(TOKENS).astype(jnp.int32)


def with_ends(values, stream_key, least, largest):
    longest = values.shape.index(max(values.shape))
    spots = []
    for shift in (0, 1):
        where = [jax.random.randint(jax.random.fold_in(stream_key, axis), (), 0, length) for axis, length in enumerate(values.shape)]
        where[longest] = (where[longest] + shift) % values.shape[longest]
        spots.append(tuple(where))
    return values.at[spots[0]].set(least).at[spots[1]].set(largest)


def levels(rng, extent, cuts, smallest, largest):
    def one(position, parts):
        draws = jax.random.uniform(jax.random.fold_in(jax.random.fold_in(rng, 6), position), (parts,), jnp.float32, smallest / len(cuts), largest / len(cuts))
        return jnp.repeat(jnp.exp(draws), extent[position] // parts).reshape((-1,) + (1,) * (len(extent) - position - 1))

    gain = one(*cuts[0])
    for cut in cuts[1:]:
        gain = gain * one(*cut)
    return gain


def centred(stream_key, dims, spread, bound, cuts=(), held_as=jnp.bfloat16):
    drawn = jax.random.normal(stream_key, dims, jnp.float32) * spread
    if len(cuts) > 0:
        drawn = levels(stream_key, dims, cuts, -0.22, 0.18) * drawn
    return jnp.clip(drawn, min=-bound, max=bound).astype(held_as)


def setup_inputs(seed: int = 0) -> dict:
    streams_of = jax.random.split(jax.random.key(seed), 8)
    return {
        "activations": centred(streams_of[0], (TOKENS, D), 1.0, 6.0, ((0, 256),)),
        "gate_weights": centred(streams_of[1], (2 * EXPERTS, D // 2, H), D ** -0.5, 0.09375, ((0, 256),)),
        "up_weights": centred(streams_of[2], (2 * EXPERTS, D // 2, H), D ** -0.5, 0.09375, ((0, 256),)),
        "down_weights": centred(streams_of[3], (2 * EXPERTS, H, D // 2), (H // 4) ** -0.5, 0.375, ((0, 256),)),
        "expert_ids": draw_expert_ids(jax.random.fold_in(streams_of[7], 71), 0),
        "gate_scores": with_ends(jax.random.randint(streams_of[5], (TOKENS, TOPK), 1, 16), jax.random.fold_in(streams_of[5], 1), 1, 15).astype(jnp.int32),
        "arrival_pos": draw_arrival_pos(jax.random.fold_in(streams_of[7], 71), 0),
    }


def reference(activations, gate_weights, up_weights, down_weights, expert_ids, gate_scores, arrival_pos):
    blocks = TOKENS // TOK_DEV
    half_width = D // 2
    token_index = jnp.arange(TOKENS, dtype=jnp.int32)
    block_of = token_index // TOK_DEV
    flat_expert = expert_ids.reshape(-1).astype(jnp.int32)
    flat_block = jnp.repeat(block_of, TOPK)
    flat_arrival = jnp.repeat(arrival_pos.astype(jnp.int32), TOPK)
    counts = jnp.zeros((blocks, EXPERTS, TOK_DEV), jnp.int32).at[flat_block, flat_expert, flat_arrival].add(1)
    before = (jnp.cumsum(counts, axis=0) - counts).astype(jnp.int32)
    totals = jnp.sum(counts, axis=0).astype(jnp.int32)
    earlier = (jnp.cumsum(totals, axis=1) - totals).astype(jnp.int32)
    flat_rank = (earlier[flat_expert, flat_arrival] + before[flat_block, flat_expert, flat_arrival]).astype(jnp.int32)
    pick_rank = flat_rank.reshape(TOKENS, TOPK)
    kept_mask = (pick_rank < CAP).astype(jnp.int32)
    kept_scores = gate_scores * kept_mask
    weight_sum = jnp.maximum(jnp.sum(kept_scores, axis=1), 1)
    routing = kept_scores.astype(jnp.float32) / weight_sum.astype(jnp.float32)[:, None]
    slot_target = jnp.where(kept_mask.reshape(-1) > 0, flat_rank, CAP).astype(jnp.int32)
    flat_token = jnp.repeat(token_index, TOPK)
    slot_token = jnp.zeros((EXPERTS, CAP), jnp.int32).at[flat_expert, slot_target].set(flat_token, mode="drop")
    slot_route = jnp.zeros((EXPERTS, CAP), jnp.float32).at[flat_expert, slot_target].set(routing.reshape(-1), mode="drop")

    def one_expert(accumulated, expert_index):
        picked = activations[slot_token[expert_index]]
        picked = jnp.where((slot_route[expert_index] > 0)[:, None], picked, jnp.zeros_like(picked))
        gate_parts = []
        up_parts = []
        for h in range(2):
            columns = picked[:, h * half_width:(h + 1) * half_width]
            gate_parts.append(jnp.dot(columns, gate_weights[2 * expert_index + h], preferred_element_type=jnp.float32).astype(jnp.bfloat16))
            up_parts.append(jnp.dot(columns, up_weights[2 * expert_index + h], preferred_element_type=jnp.float32).astype(jnp.bfloat16))
        gate_sum = gate_parts[0].astype(jnp.float32) + gate_parts[1].astype(jnp.float32)
        up_sum = up_parts[0].astype(jnp.float32) + up_parts[1].astype(jnp.float32)
        hidden = (jax.nn.silu(gate_sum) * up_sum).astype(jnp.bfloat16)
        outputs = []
        for h in range(2):
            outputs.append(jnp.dot(hidden, down_weights[2 * expert_index + h], preferred_element_type=jnp.float32).astype(jnp.bfloat16))
        expert_out = jnp.concatenate(outputs, axis=1).astype(jnp.float32)
        accumulated = accumulated.at[slot_token[expert_index]].add(slot_route[expert_index][:, None] * expert_out)
        return accumulated, None

    def one_group(total, group_index):
        def member_step(accumulated, member):
            return one_expert(accumulated, group_index * EXP_GROUP + member)

        part, unused = lax.scan(member_step, jnp.zeros((TOKENS, D), jnp.float32), jnp.arange(EXP_GROUP, dtype=jnp.int32))
        rounded = lax.optimization_barrier(part.astype(jnp.bfloat16)).astype(jnp.float32)
        return total + rounded, None

    summed, unused = lax.scan(one_group, jnp.zeros((TOKENS, D), jnp.float32), jnp.arange(EXPERTS // EXP_GROUP, dtype=jnp.int32))
    return summed.astype(jnp.bfloat16)
```

```python
import functools

import jax
import jax.numpy as jnp
from jax import lax
from jax.experimental import pallas as pl
from jax.experimental.pallas import tpu as pltpu
from jax.sharding import PartitionSpec as P

TOPG = 4
META = 128
AT_SCORE, AT_POS, AT_ONE = 8, 16, 17
EMPTY = 1.0e9
NEAR = (0, -1, 1, -2)
FAR = (2, -3, 3, -4)
F32, BF16 = jnp.float32, jnp.bfloat16


def iota(shape, axis):
    return lax.broadcasted_iota(jnp.int32, shape, axis)


def divided(value, by, most):
    total = jnp.zeros_like(value)
    for j in range(1, most):
        total = total + (value >= j * by).astype(jnp.int32)
    return total


def tiles(width, tile):
    return [(at, min(tile, width - at)) for at in range(0, width, tile)]


def call(kernel, name, out_shape, flops, moved, vmem, **more):
    return pl.pallas_call(
        kernel,
        out_shape=out_shape,
        name=name,
        cost_estimate=pl.CostEstimate(flops=flops, bytes_accessed=moved, transcendentals=0),
        compiler_params=pltpu.CompilerParams(vmem_limit_bytes=vmem << 20),
        **more,
    )


def pick_rows_kernel(place_ref, *refs, groups, per_group, slots):
    blocks, out_ref = refs[:-1], refs[-1]
    tok, width = blocks[0].shape
    feat = width - META
    total = tok * len(blocks)
    rows = slots * len(blocks)
    meta = jnp.concatenate([b[:, feat:] for b in blocks], axis=0)
    unit = (iota((32, META), 0) == iota((32, META), 1)).astype(F32).astype(BF16)
    meta_t = lax.dot_general(unit, meta, (((1,), (1,)), ((), ())), preferred_element_type=F32)
    expert = (iota((groups, total), 0) * per_group + place_ref[0]).astype(F32)
    hit = jnp.zeros((groups, total), F32)
    for k in range(AT_SCORE):
        hit = hit + (meta_t[k : k + 1, :] == expert).astype(F32)
    first, second = iota((total, total), 0), iota((total, total), 1)
    same = divided(first, tok, len(blocks)) == divided(second, tok, len(blocks))
    before = (same & (first < second)).astype(F32).astype(BF16)
    occurrence = jnp.dot(hit.astype(BF16), before, preferred_element_type=F32)
    block_of = divided(iota((groups, total), 1), tok, len(blocks)).astype(F32)
    slot = jnp.where(hit > 0, occurrence + slots * block_of, -1.0)
    slot = jnp.broadcast_to(slot[:, None, :], (groups, rows, total))
    chosen = (slot == iota((groups, rows, total), 1).astype(F32)).astype(F32)
    chosen = chosen.reshape(groups * rows, total).astype(BF16)
    for at, wide in tiles(width, 512):
        part = jnp.concatenate([b[:, at : at + wide] for b in blocks], axis=0)
        out_ref[:, at : at + wide] = jnp.dot(chosen, part, preferred_element_type=F32).astype(BF16)


def pick_rows(place, blocks, groups, per_group, slots):
    width = blocks[0].shape[1]
    total = blocks[0].shape[0] * len(blocks)
    rows = groups * slots * len(blocks)
    return call(
        functools.partial(pick_rows_kernel, groups=groups, per_group=per_group, slots=slots),
        "pick_rows",
        jax.ShapeDtypeStruct((rows, width), BF16),
        2 * rows * total * width,
        2 * (rows + total) * width,
        40,
        in_specs=[pl.BlockSpec(memory_space=pltpu.SMEM)]
        + [pl.BlockSpec(memory_space=pltpu.VMEM)] * len(blocks),
        out_specs=pl.BlockSpec(memory_space=pltpu.VMEM),
    )(place, *blocks)


def score_table_kernel(place_ref, *refs, groups, per_group, slots):
    blocks, out_ref = refs[:-1], refs[-1]
    tok = blocks[0].shape[0]
    total = tok * len(blocks)
    rows = slots * len(blocks)
    meta = jnp.concatenate([b[...] for b in blocks], axis=0).astype(F32)
    expert = (iota((total, META), 1) * per_group + place_ref[0]).astype(F32)
    hit = jnp.zeros((total, META), F32)
    score = jnp.zeros((total, META), F32)
    for k in range(AT_SCORE):
        same = (meta[:, k : k + 1] == expert).astype(F32)
        hit = hit + same
        score = score + same * meta[:, AT_SCORE + k : AT_SCORE + k + 1]
    first, second = iota((total, total), 0), iota((total, total), 1)
    same = divided(first, tok, len(blocks)) == divided(second, tok, len(blocks))
    before = (same & (second < first)).astype(F32).astype(BF16)
    occurrence = jnp.dot(before, hit.astype(BF16), preferred_element_type=F32)
    block_of = divided(iota((total, META), 0), tok, len(blocks)).astype(F32)
    slot = jnp.where(hit > 0, occurrence + slots * block_of, -1.0)
    source, lane = iota((META, groups * rows), 0), iota((META, groups * rows), 1)
    spread = ((lane >= source * rows) & (lane < source * rows + rows)).astype(F32).astype(BF16)
    slot_wide = jnp.dot(slot.astype(BF16), spread, preferred_element_type=F32)
    score_wide = jnp.dot(score.astype(BF16), spread, preferred_element_type=F32)
    column = iota((1, groups * rows), 1)
    column = (column - rows * divided(column, rows, groups)).astype(F32)
    out_ref[...] = jnp.where(slot_wide == column, score_wide, 0.0).astype(BF16)


def score_table(place, blocks, groups, per_group, slots):
    tok, width = blocks[0].shape
    total = tok * len(blocks)
    columns = groups * slots * len(blocks)
    last = width // META - 1
    return call(
        functools.partial(score_table_kernel, groups=groups, per_group=per_group, slots=slots),
        "score_table",
        jax.ShapeDtypeStruct((total, columns), BF16),
        2 * total * columns * (2 * META),
        2 * total * columns,
        40,
        grid=(1,),
        in_specs=[pl.BlockSpec(memory_space=pltpu.SMEM)]
        + [pl.BlockSpec((tok, META), lambda i: (0, last))] * len(blocks),
        out_specs=pl.BlockSpec((total, columns), lambda i: (0, 0)),
    )(place, *blocks)


def hidden_kernel(
    place_ref, rows_ref, gate_own, gate_other, up_own, up_other, out_ref, line_ref, column_ref,
    *, groups, members, slots, offsets
):
    count = rows_ref.shape[0]
    half = gate_own.shape[1]
    z, c = place_ref[0], place_ref[1]

    @pl.when(pl.program_id(0) == 0)
    def _():
        meta = rows_ref[:, 2 * half :]
        unit = (iota((32, META), 0) == iota((32, META), 1)).astype(F32).astype(BF16)
        meta_t = lax.dot_general(unit, meta, (((1,), (1,)), ((), ())), preferred_element_type=F32)

        def key(index, position, valid):
            group = divided(index, count // groups, groups)
            block = divided(index - (count // groups) * group, slots, len(offsets))
            apart = jnp.zeros_like(index)
            for j, offset in enumerate(offsets):
                apart = apart + jnp.where(block == j, offset, 0)
            ring = members // 2
            where = z + apart
            where = jnp.where(where < 0, where + ring, where)
            where = jnp.where(where >= ring, where - ring, where)
            source = (group * members + where * 2 + c).astype(F32)
            return jnp.where(valid > 0, position * (groups * members) + source, EMPTY)

        line = key(iota((1, count), 1), meta_t[AT_POS : AT_POS + 1], meta_t[AT_ONE : AT_ONE + 1])
        line_ref[...] = jnp.broadcast_to(line, line_ref.shape)
        wide = meta.astype(F32)
        column = key(
            iota((count, 1), 0), wide[:, AT_POS : AT_POS + 1], wide[:, AT_ONE : AT_ONE + 1]
        )
        column_ref[...] = jnp.broadcast_to(column, column_ref.shape)

    own = rows_ref[:, pl.ds(pl.multiple_of(c * half, 128), half)]
    other = rows_ref[:, pl.ds(pl.multiple_of((1 - c) * half, 128), half)]
    gate = jnp.dot(own, gate_own[0], preferred_element_type=F32) + jnp.dot(
        other, gate_other[0], preferred_element_type=F32
    )
    up = jnp.dot(own, up_own[0], preferred_element_type=F32) + jnp.dot(
        other, up_other[0], preferred_element_type=F32
    )
    out_ref[...] = (gate / (1.0 + jnp.exp(-gate)) * up).astype(BF16)


def hidden_rows(place, rows, gate_own, gate_other, up_own, up_other, groups, members, slots, offsets):
    count, width = rows.shape
    half, units = gate_own.shape[1:]
    tile = 256
    weight = pl.BlockSpec((1, half, tile), lambda i: (0, 0, i))
    return call(
        functools.partial(
            hidden_kernel, groups=groups, members=members, slots=slots, offsets=offsets
        ),
        "hidden_rows",
        (
            jax.ShapeDtypeStruct((count, units), BF16),
            jax.ShapeDtypeStruct((8, count), F32),
            jax.ShapeDtypeStruct((count, META), F32),
        ),
        8 * count * half * units,
        2 * (count * width + 4 * half * units + count * units),
        40,
        grid=(units // tile,),
        in_specs=[
            pl.BlockSpec(memory_space=pltpu.SMEM),
            pl.BlockSpec((count, width), lambda i: (0, 0)),
            weight,
            weight,
            weight,
            weight,
        ],
        out_specs=(
            pl.BlockSpec((count, tile), lambda i: (0, i)),
            pl.BlockSpec((8, count), lambda i: (0, 0)),
            pl.BlockSpec((count, META), lambda i: (0, 0)),
        ),
    )(place, rows, gate_own, gate_other, up_own, up_other)


def down_tiles(hidden_ref, weight_ref, out_ref, tile):
    def step(i, carry):
        columns = pl.ds(pl.multiple_of(i * tile, 128), tile)
        out_ref[:, columns] = jnp.dot(
            hidden_ref[...], weight_ref[0, :, columns], preferred_element_type=F32
        ).astype(BF16)
        return carry

    lax.fori_loop(0, weight_ref.shape[2] // tile, step, 0)


def down_first_kernel(*refs, parts, groups, capacity):
    lines, columns, hiddens = refs[: 2 * parts], refs[2 * parts : 3 * parts], refs[3 * parts : 4 * parts]
    weight_ref, out_ref, all_ref, flag_ref = refs[4 * parts :]
    masked, flags = [], []
    for column_ref, hidden_ref in zip(columns, hiddens):
        own = column_ref[:, :1]
        rank = jnp.zeros(own.shape, F32)
        for line_ref in lines:
            rank = rank + jnp.sum((line_ref[:1, :] < own).astype(F32), axis=1, keepdims=True)
        kept = jnp.where((rank < capacity) & (own < EMPTY), 1.0, 0.0)
        masked.append(hidden_ref[...].astype(F32) * kept)
        flags.append(jnp.broadcast_to(kept, (kept.shape[0], META)))
    part = masked[0].shape[0] // groups
    rows = part * parts
    for g in range(groups):
        cut = slice(g * part, (g + 1) * part)
        to = slice(g * rows, (g + 1) * rows)
        all_ref[to, :] = jnp.concatenate([m[cut] for m in masked], axis=0).astype(BF16)
        flag_ref[to, :] = jnp.concatenate([f[cut] for f in flags], axis=0).astype(BF16)
    down_tiles(all_ref, weight_ref, out_ref, 256)


def down_first(lines, columns, hiddens, weight, groups, capacity):
    count = sum(h.shape[0] for h in hiddens)
    units, half = weight.shape[1:]
    return call(
        functools.partial(
            down_first_kernel, parts=len(hiddens), groups=groups, capacity=capacity
        ),
        "down_first",
        (
            jax.ShapeDtypeStruct((count, half), BF16),
            jax.ShapeDtypeStruct((count, units), BF16),
            jax.ShapeDtypeStruct((count, META), BF16),
        ),
        2 * count * half * units,
        2 * (count * (half + units) + half * units),
        48,
        in_specs=[pl.BlockSpec(memory_space=pltpu.VMEM)] * (4 * len(hiddens) + 1),
        out_specs=(pl.BlockSpec(memory_space=pltpu.VMEM),) * 3,
    )(*lines, *columns, *hiddens, weight)


def down_second_kernel(hidden_ref, flag_ref, weight_ref, out_ref):
    half = weight_ref.shape[2]
    down_tiles(hidden_ref, weight_ref, out_ref, 256)
    out_ref[:, half:] = flag_ref[...]


def down_second(hidden, flags, weight):
    count = hidden.shape[0]
    units, half = weight.shape[1:]
    return call(
        down_second_kernel,
        "down_second",
        jax.ShapeDtypeStruct((count, half + META), BF16),
        2 * count * half * units,
        2 * (count * (half + units) + half * units),
        40,
        in_specs=[pl.BlockSpec(memory_space=pltpu.VMEM)] * 3,
        out_specs=pl.BlockSpec(memory_space=pltpu.VMEM),
    )(hidden, flags, weight)


def combine_kernel(table_ref, rows_ref, *out_refs):
    tok = out_refs[0].shape[0]
    for at, wide in tiles(rows_ref.shape[1], 512):
        part = jnp.dot(table_ref[...], rows_ref[:, at : at + wide], preferred_element_type=F32)
        for b, out_ref in enumerate(out_refs):
            out_ref[:, at : at + wide] = part[b * tok : (b + 1) * tok].astype(BF16)


def combine(table, rows, blocks):
    total, count = table.shape
    width = rows.shape[1]
    return call(
        combine_kernel,
        "combine",
        (jax.ShapeDtypeStruct((total // blocks, width), BF16),) * blocks,
        2 * total * count * width,
        2 * (total * count + (count + total) * width),
        40,
        in_specs=[pl.BlockSpec(memory_space=pltpu.VMEM)] * 2,
        out_specs=(pl.BlockSpec(memory_space=pltpu.VMEM),) * blocks,
    )(table, rows)


def per_device(
    activations, gate_weights, up_weights, down_weights, expert_ids, gate_scores, arrival_pos
):
    groups = lax.axis_size("group")
    members = lax.axis_size("ingroup")
    per_group = ring = members // 2
    tok = activations.shape[0]
    model = activations.shape[1]
    half = model // 2
    top_picks = expert_ids.shape[1]
    capacity = 2 * top_picks * tok
    group_most = min(tok, 3 * tok * TOPG // (2 * groups))
    slots = (2 * group_most + per_group - 1) // per_group
    index = lax.axis_index("ingroup")
    place = jnp.stack([index // 2, index % 2]).astype(jnp.int32)
    partner = [(i, i ^ 1) for i in range(members)]

    def along(shard, by):
        hop = [(i, (i // 2 + by) % ring * 2 + i % 2) for i in range(members)]
        return lax.ppermute(shard, "ingroup", hop)

    def swap(shard):
        return lax.ppermute(shard, "ingroup", partner)

    def exchange(rows):
        return lax.all_to_all(rows, "group", split_axis=0, concat_axis=0, tiled=True)

    extra = jnp.concatenate(
        [
            expert_ids,
            gate_scores,
            arrival_pos[:, None],
            jnp.ones((tok, 1), jnp.int32),
            jnp.zeros((tok, META - 2 * top_picks - 2), jnp.int32),
        ],
        axis=1,
    )
    held = {0: jnp.concatenate([activations, extra.astype(BF16)], axis=1)}
    for step in range(1, ring // 2 + 1):
        held[-step] = along(held[1 - step], 1)
        if step < ring // 2:
            held[step] = along(held[step - 1], -1)
    gate_other, up_other, down_other = swap(gate_weights), swap(up_weights), swap(down_weights)

    lines, columns, hiddens = [], [], []
    for offsets in (NEAR, FAR):
        rows = exchange(
            pick_rows(place, [held[o] for o in offsets], groups, per_group, slots)
        )
        hidden, line, column = hidden_rows(
            place, rows, gate_weights, gate_other, up_weights, up_other,
            groups, members, slots, offsets,
        )
        lines.append(line)
        columns.append(column)
        hiddens.append(hidden)
    order = NEAR + FAR
    table = score_table(place, [held[o] for o in order], groups, per_group, slots)
    lines = lines + [swap(line) for line in lines]
    own_out, hidden, flags = down_first(lines, columns, hiddens, down_weights, groups, capacity)
    other_out = down_second(hidden, flags, down_other)

    halves = []
    for out in (own_out, other_out):
        parts = dict(zip(order, combine(table, exchange(out), len(order))))
        sums = [parts[0].astype(F32)]
        for way in (-1, 1):
            most = ring // 2 if way == -1 else ring // 2 - 1
            moving = parts[way * most]
            for step in range(most - 1, 0, -1):
                moving = along(moving, way)
                moving = (moving.astype(F32) + parts[way * step].astype(F32)).astype(BF16)
            sums.append(along(moving, way).astype(F32))
        halves.append(sum(sums))
    weight_sum = jnp.maximum(halves[1][:, half : half + 1], 1.0)
    own, other = halves[0] / weight_sum, halves[1][:, :half] / weight_sum
    is_first = index % 2 == 0
    left = jnp.where(is_first, own, other)
    right = jnp.where(is_first, other, own)
    return jnp.concatenate([left, right], axis=1).astype(BF16)


def solution(mesh):
    rows = P(("group", "ingroup"), None)
    weights = P(("group", "ingroup"), None, None)
    return jax.shard_map(
        per_device,
        mesh=mesh,
        in_specs=(rows, weights, weights, weights, rows, rows, P(("group", "ingroup"))),
        out_specs=rows,
        check_vma=False,
    )
```

```python
import functools

import jax
import jax.numpy as jnp
from jax import lax
from jax.experimental import pallas as pl
from jax.experimental.pallas import tpu as pltpu
from jax.sharding import PartitionSpec as P

TOPG = 4
META = 128
AT_SCORE, AT_POS, AT_ONE = 8, 16, 17
EMPTY = 1.0e9
NEAR = (0, -1, 1, -2)
FAR = (2, -3, 3, -4)
F32, BF16 = jnp.float32, jnp.bfloat16


def iota(shape, axis):
    return lax.broadcasted_iota(jnp.int32, shape, axis)


def divided(value, by, most):
    total = jnp.zeros_like(value)
    for j in range(1, most):
        total = total + (value >= j * by).astype(jnp.int32)
    return total


def tiles(width, tile):
    return [(at, min(tile, width - at)) for at in range(0, width, tile)]


def call(kernel, name, out_shape, flops, moved, vmem, **more):
    return pl.pallas_call(
        kernel,
        out_shape=out_shape,
        name=name,
        cost_estimate=pl.CostEstimate(flops=flops, bytes_accessed=moved, transcendentals=0),
        compiler_params=pltpu.CompilerParams(vmem_limit_bytes=vmem << 20),
        **more,
    )


WHOLE = pl.BlockSpec(memory_space=pltpu.VMEM)
SCALARS = pl.BlockSpec(memory_space=pltpu.SMEM)


STAYS = pl.BlockSpec(memory_space=pltpu.HBM)


def far_memory(*arrays):
    return [pltpu.with_memory_space_constraint(a, pltpu.HBM) for a in arrays]


def unit(rows):
    return (iota((rows, META), 0) == iota((rows, META), 1)).astype(F32).astype(BF16)


def lines_of(columns, rows):
    return lax.dot_general(
        unit(rows), columns, (((1,), (1,)), ((), ())), preferred_element_type=F32
    )


def start_rows_kernel(rows_ref, ids_ref, scores_ref, pos_ref, left_ref, right_ref):
    half = left_ref.shape[1]
    tok = rows_ref.shape[0]
    lines = [ids_ref[...].astype(F32), scores_ref[...].astype(F32), pos_ref[...].astype(F32)]
    lines.append(jnp.ones((1, tok), F32))
    lines.append(jnp.zeros((14, tok), F32))
    lines = jnp.concatenate(lines, axis=0).astype(BF16)
    meta = lax.dot_general(lines, unit(32), (((0,), (0,)), ((), ())), preferred_element_type=F32)
    left_ref[...] = rows_ref[:, :half]
    right_ref[:, :half] = rows_ref[:, half:]
    right_ref[:, half:] = meta.astype(BF16)


def start_rows(rows, ids, scores, pos):
    tok, model = rows.shape
    half = model // 2
    return call(
        start_rows_kernel,
        "start_rows",
        (jax.ShapeDtypeStruct((tok, half), BF16), jax.ShapeDtypeStruct((tok, half + META), BF16)),
        0,
        4 * tok * model,
        4,
        grid=(1,),
        in_specs=[
            pl.BlockSpec(a.shape, lambda i: (0, 0)) for a in (rows, ids.T, scores.T, pos[None, :])
        ],
        out_specs=(
            pl.BlockSpec((tok, half), lambda i: (0, 0)),
            pl.BlockSpec((tok, half + META), lambda i: (0, 0)),
        ),
    )(*far_memory(rows, ids.T, scores.T, pos[None, :]))


def pick_rows_kernel(place_ref, *refs, groups, per_group, slots, first_block, first_row, rows):
    out_ref, meta_ref, built_ref, sent = refs[-4:]
    count = (len(refs) - 4) // 2
    lefts, rights = refs[:count], refs[count:-4]
    copies = []
    tok, half = lefts[0].shape
    total = tok * count
    meta = jnp.concatenate([b[:, half:] for b in rights], axis=0)
    meta_ref[...] = meta
    meta_t = lines_of(meta, 32)
    expert = (iota((groups, total), 0) * per_group + place_ref[0]).astype(F32)
    hit = jnp.zeros((groups, total), F32)
    for k in range(AT_SCORE):
        hit = hit + (meta_t[k : k + 1, :] == expert).astype(F32)
    first, second = iota((total, total), 0), iota((total, total), 1)
    same = divided(first, tok, count) == divided(second, tok, count)
    before = (same & (first < second)).astype(F32).astype(BF16)
    occurrence = jnp.dot(hit.astype(BF16), before, preferred_element_type=F32)
    block_of = divided(iota((groups, total), 1), tok, count).astype(F32)
    slot = occurrence + slots * (block_of + first_block) - first_row
    slot = jnp.where(hit > 0, slot, -1.0)
    slot = jnp.broadcast_to(slot[:, None, :], (groups, rows, total))
    chosen = (slot == iota((groups, rows, total), 1).astype(F32)).astype(F32)
    chosen = chosen.reshape(groups * rows, total).astype(BF16)
    for start, blocks in ((0, lefts), (half, rights)):
        for at, wide in tiles(blocks[0].shape[1], 512):
            part = jnp.concatenate([b[:, at : at + wide] for b in blocks], axis=0)
            cut = pl.ds(start + at, wide)
            built_ref[:, cut] = jnp.dot(chosen, part, preferred_element_type=F32).astype(BF16)
            copies.append(
                pltpu.make_async_copy(built_ref.at[:, cut], out_ref.at[:, cut], sent.at[len(copies)])
            )
            copies[-1].start()
    for copy in copies:
        copy.wait()


def pick_rows(place, lefts, rights, groups, per_group, slots, first_block, first_row, rows):
    width = lefts[0].shape[1] + rights[0].shape[1]
    total = lefts[0].shape[0] * len(lefts)
    return call(
        functools.partial(
            pick_rows_kernel, groups=groups, per_group=per_group, slots=slots,
            first_block=first_block, first_row=first_row, rows=rows,
        ),
        "pick_rows",
        (pltpu.HBM((groups * rows, width), BF16), jax.ShapeDtypeStruct((total, META), BF16)),
        2 * groups * rows * total * width,
        2 * (groups * rows + total) * width,
        12,
        in_specs=[SCALARS] + [WHOLE] * (2 * len(lefts)),
        out_specs=(STAYS, WHOLE),
        scratch_shapes=[pltpu.VMEM((groups * rows, width), BF16), pltpu.SemaphoreType.DMA((8,))],
    )(place, *lefts, *rights)


def score_table_kernel(place_ref, meta_ref, out_ref, *, groups, per_group, slots, blocks):
    total = meta_ref.shape[0]
    tok = total // blocks
    rows = slots * blocks
    meta = meta_ref[...].astype(F32)
    expert = (iota((total, META), 1) * per_group + place_ref[0]).astype(F32)
    hit = jnp.zeros((total, META), F32)
    score = jnp.zeros((total, META), F32)
    for k in range(AT_SCORE):
        same = (meta[:, k : k + 1] == expert).astype(F32)
        hit = hit + same
        score = score + same * meta[:, AT_SCORE + k : AT_SCORE + k + 1]
    first, second = iota((total, total), 0), iota((total, total), 1)
    same = divided(first, tok, blocks) == divided(second, tok, blocks)
    before = (same & (second < first)).astype(F32).astype(BF16)
    occurrence = jnp.dot(before, hit.astype(BF16), preferred_element_type=F32)
    block_of = divided(iota((total, META), 0), tok, blocks).astype(F32)
    slot = jnp.where(hit > 0, occurrence + slots * block_of, -1.0)
    source, lane = iota((META, groups * rows), 0), iota((META, groups * rows), 1)
    spread = ((lane >= source * rows) & (lane < source * rows + rows)).astype(F32).astype(BF16)
    slot_wide = jnp.dot(slot.astype(BF16), spread, preferred_element_type=F32)
    score_wide = jnp.dot(score.astype(BF16), spread, preferred_element_type=F32)
    column = iota((1, groups * rows), 1)
    column = (column - rows * divided(column, rows, groups)).astype(F32)
    out_ref[...] = jnp.where(slot_wide == column, score_wide, 0.0).astype(BF16)


def score_table(place, meta, groups, per_group, slots, blocks):
    total = meta.shape[0]
    columns = groups * slots * blocks
    return call(
        functools.partial(
            score_table_kernel, groups=groups, per_group=per_group, slots=slots, blocks=blocks
        ),
        "score_table",
        pltpu.HBM((total, columns), BF16),
        2 * total * columns * (2 * META),
        2 * total * columns,
        12,
        grid=(1,),
        in_specs=[SCALARS, pl.BlockSpec((total, META), lambda i: (0, 0))],
        out_specs=pl.BlockSpec((total, columns), lambda i: (0, 0)),
    )(place, meta)


def slot_keys_kernel(place_ref, *refs, groups, members, slots, offsets):
    meta_refs, (line_ref, column_ref) = refs[:-2], refs[-2:]
    z, c = place_ref[0], place_ref[1]
    rows = line_ref.shape[1] // groups
    first = 0
    for meta_ref in meta_refs:
        count = meta_ref.shape[0]
        part = count // groups
        meta = meta_ref[...]
        meta_t = lines_of(meta, 32)

        def key(index, position, valid):
            group = divided(index, part, groups)
            block = divided(index - part * group + first, slots, len(offsets))
            apart = jnp.zeros_like(index)
            for j, offset in enumerate(offsets):
                apart = apart + jnp.where(block == j, offset, 0)
            ring = members // 2
            where = z + apart
            where = jnp.where(where < 0, where + ring, where)
            where = jnp.where(where >= ring, where - ring, where)
            source = (group * members + where * 2 + c).astype(F32)
            return jnp.where(valid > 0, position * (groups * members) + source, EMPTY)

        line = key(iota((1, count), 1), meta_t[AT_POS : AT_POS + 1], meta_t[AT_ONE : AT_ONE + 1])
        at = first * groups
        line_ref[:, at : at + count] = jnp.broadcast_to(line, (line_ref.shape[0], count))
        wide = meta.astype(F32)
        column = key(
            iota((count, 1), 0), wide[:, AT_POS : AT_POS + 1], wide[:, AT_ONE : AT_ONE + 1]
        )
        column = jnp.broadcast_to(column, meta.shape)
        for g in range(groups):
            at = g * rows + first
            column_ref[at : at + part, :] = column[g * part : (g + 1) * part]
        first += part


def slot_keys(place, parts, groups, members, slots, offsets):
    count = sum(rows.shape[0] for rows in parts)
    last = parts[0].shape[1] // META - 1
    return call(
        functools.partial(
            slot_keys_kernel, groups=groups, members=members, slots=slots, offsets=offsets
        ),
        "slot_keys",
        (jax.ShapeDtypeStruct((8, count), F32), jax.ShapeDtypeStruct((count, META), F32)),
        0,
        16 * count * META,
        4,
        grid=(1,),
        in_specs=[SCALARS]
        + [pl.BlockSpec((rows.shape[0], META), lambda i: (0, last)) for rows in parts],
        out_specs=(
            pl.BlockSpec((8, count), lambda i: (0, 0)),
            pl.BlockSpec((count, META), lambda i: (0, 0)),
        ),
    )(place, *parts)


def kept_flags(lines, columns, capacity):
    count = columns[0].shape[0]
    lane = iota((count, META), 1)
    flags = jnp.zeros((count, META), F32)
    for q, column_ref in enumerate(columns):
        own = column_ref[:, :1]
        rank = jnp.zeros(own.shape, F32)
        for line_ref in lines:
            rank = rank + jnp.sum((line_ref[:1, :] < own).astype(F32), axis=1, keepdims=True)
        kept = jnp.where((rank < capacity) & (own < EMPTY), 1.0, 0.0)
        flags = jnp.where(lane == q, kept, flags)
    return flags.astype(BF16)


def expert_kernel(
    place_ref, gate_own, gate_other, up_own, up_other, down_own, down_other, *refs, lines, capacity
):
    line_refs, refs = refs[:lines], refs[lines:]
    column_refs, refs = refs[: lines // 2], refs[lines // 2 :]
    came_ref, out_ref, total_ref, rows_ref, came = refs
    half = gate_own.shape[1]
    c = place_ref[1]
    step = pl.program_id(0)

    @pl.when(step == 0)
    def _():
        copy = pltpu.make_async_copy(came_ref, rows_ref, came)
        copy.start()
        if lines:
            out_ref[:, 2 * half :] = kept_flags(line_refs, column_refs, capacity)
        copy.wait()

    own = rows_ref[:, pl.ds(pl.multiple_of(c * half, 128), half)]
    other = rows_ref[:, pl.ds(pl.multiple_of((1 - c) * half, 128), half)]
    gate = jnp.dot(own, gate_own[0], preferred_element_type=F32) + jnp.dot(
        other, gate_other[0], preferred_element_type=F32
    )
    up = jnp.dot(own, up_own[0], preferred_element_type=F32) + jnp.dot(
        other, up_other[0], preferred_element_type=F32
    )
    hidden = (gate / (1.0 + jnp.exp(-gate)) * up).astype(BF16)
    for at, down in ((0, down_own), (half, down_other)):
        part = jnp.dot(hidden, down[0], preferred_element_type=F32)
        cut = slice(at, at + half)

        @pl.when(step == 0)
        def _():
            total_ref[:, cut] = part

        @pl.when((step > 0) & (step < pl.num_programs(0) - 1))
        def _():
            total_ref[:, cut] = total_ref[:, cut] + part

        @pl.when(step == pl.num_programs(0) - 1)
        def _():
            out_ref[:, cut] = (total_ref[:, cut] + part).astype(BF16)


def expert(place, rows, weights, lines, columns, capacity):
    count, width = rows.shape
    half, units = weights[0].shape[1:]
    tile = 256
    weight = pl.BlockSpec((1, half, tile), lambda i: (0, 0, i))
    down = pl.BlockSpec((1, tile, half), lambda i: (0, i, 0))
    out = 2 * half + (META if lines else 0)
    return call(
        functools.partial(expert_kernel, lines=len(lines), capacity=capacity),
        "expert",
        pltpu.HBM((count, out), BF16),
        12 * count * half * units,
        2 * (count * width + 6 * half * units + count * out),
        44,
        grid=(units // tile,),
        in_specs=[SCALARS]
        + [weight] * 4
        + [down] * 2
        + [pl.BlockSpec((8, count), lambda i: (0, 0))] * len(lines)
        + [pl.BlockSpec((count, META), lambda i: (0, 0))] * len(columns)
        + [STAYS],
        out_specs=pl.BlockSpec((count, out), lambda i: (0, 0)),
        scratch_shapes=[
            pltpu.VMEM((count, 2 * half), F32),
            pltpu.VMEM((count, width), BF16),
            pltpu.SemaphoreType.DMA,
        ],
    )(place, *far_memory(*weights), *lines, *columns, *far_memory(rows))


def combine_kernel(table_ref, flag_ref, *refs, parts, pieces, groups, flag):
    part_refs, out_refs = refs[:parts], refs[parts : -parts - 2]
    kept_refs, built_ref, sent = refs[-parts - 2 : -2], refs[-2], refs[-1]
    tile = part_refs[0].shape[1]
    tok = out_refs[0].shape[0]
    blocks = len(out_refs) // pieces
    step, steps = pl.program_id(0), pl.num_programs(0)
    half = out_refs[-1].shape[1]

    @pl.when(step == 0)
    def _():
        table = table_ref[...].astype(F32) * lines_of(flag_ref[...], 8)[flag : flag + 1]
        total = jnp.sum(table, axis=1, keepdims=True)
        built_ref[:, 2 * half :] = jnp.broadcast_to(total, (blocks * tok, META)).astype(BF16)
        table = table.astype(BF16)
        columns = table.shape[1]
        first = 0
        for kept_ref in kept_refs:
            count = kept_ref.shape[1]
            part = count // groups
            if count == columns:
                kept_ref[...] = table
            else:
                source, lane = iota((columns, count), 0), iota((columns, count), 1)
                group = divided(lane, part, groups)
                taken = source == (columns // groups - part) * group + lane + first
                taken = taken.astype(F32).astype(BF16)
                kept_ref[...] = jnp.dot(table, taken, preferred_element_type=F32).astype(BF16)
            first += part

    total = None
    for kept_ref, part_ref in zip(kept_refs, part_refs):
        product = jnp.dot(kept_ref[...], part_ref[...], preferred_element_type=F32)
        total = product if total is None else total + product
    built_ref[:, pl.ds(pl.multiple_of(step * tile, 128), tile)] = total.astype(BF16)

    def copies(p):
        made = []
        for b in range(blocks):
            to = out_refs[p * blocks + b]
            source = built_ref.at[pl.ds(b * tok, tok), pl.ds((pieces - 1 - p) * half, to.shape[1])]
            made.append(pltpu.make_async_copy(source, to, sent.at[p, b]))
        return made

    for p in range(pieces):

        @pl.when(step == (pieces - p) * steps // pieces - 1)
        def _():
            for copy in copies(p):
                copy.start()

    @pl.when(step == steps - 1)
    def _():
        for p in range(pieces):
            for copy in copies(p):
                copy.wait()


def combine(table, far, parts, flag, half, blocks, groups):
    total, count = table.shape
    tok = total // blocks
    tile = half // 2
    last = far.shape[1] // META - 1
    return call(
        functools.partial(combine_kernel, parts=len(parts), pieces=2, groups=groups, flag=flag),
        "combine",
        (pltpu.HBM((tok, half + META), BF16),) * blocks + (pltpu.HBM((tok, half), BF16),) * blocks,
        4 * total * count * half,
        4 * (total * count + (count + total) * half),
        16,
        grid=(2 * half // tile,),
        in_specs=[
            pl.BlockSpec((total, count), lambda i: (0, 0)),
            pl.BlockSpec((count, META), lambda i: (0, last)),
        ]
        + [pl.BlockSpec((rows.shape[0], tile), lambda i: (0, i)) for rows in parts],
        out_specs=(STAYS,) * (2 * blocks),
        scratch_shapes=[pltpu.VMEM((total, rows.shape[0]), BF16) for rows in parts]
        + [
            pltpu.VMEM((total, 2 * half + META), BF16),
            pltpu.SemaphoreType.DMA((2, blocks)),
        ],
    )(*far_memory(table), far, *parts)


def per_device(
    activations, gate_weights, up_weights, down_weights, expert_ids, gate_scores, arrival_pos
):
    groups = lax.axis_size("group")
    members = lax.axis_size("ingroup")
    per_group = ring = members // 2
    tok = activations.shape[0]
    half = activations.shape[1] // 2
    top_picks = expert_ids.shape[1]
    capacity = 2 * top_picks * tok
    group_most = min(tok, 3 * tok * TOPG // (2 * groups))
    slots = (2 * group_most + per_group - 1) // per_group
    index = lax.axis_index("ingroup")
    place = jnp.stack([index // 2, index % 2]).astype(jnp.int32)
    partner = [(i, i ^ 1) for i in range(members)]

    def along(shard, by):
        hop = [(i, (i // 2 + by) % ring * 2 + i % 2) for i in range(members)]
        return lax.ppermute(shard, "ingroup", hop)

    def swap(shard):
        return lax.ppermute(shard, "ingroup", partner)

    def exchange(rows):
        return lax.all_to_all(rows, "group", split_axis=0, concat_axis=0, tiled=True)

    def gathered(shard, way):
        held = {0: shard}
        for step in range(1, ring // 2):
            held[-step] = along(held[1 - step], 1)
            held[step] = along(held[step - 1], -1)
        held[-ring // 2] = along(held[way * (ring // 2 - 1)], -way)
        return held

    def added(moving, part):
        return (moving.astype(F32) + part.astype(F32)).astype(BF16)

    def scattered(parts, way):
        sums = parts[0].astype(F32)
        for side in (way, -way):
            steps = [side * step for step in range(ring // 2 - 1, 0, -1)]
            moving = parts[-ring // 2] if side == way else parts[steps.pop(0)]
            for step in steps:
                moving = added(along(moving, side), parts[step])
            sums = sums + along(moving, side).astype(F32)
        return sums

    left, right = start_rows(activations, expert_ids, gate_scores, arrival_pos)
    lefts, rights = gathered(left, -1), gathered(right, 1)
    rows = slots * len(NEAR)
    blocks = len(NEAR)

    def picked(offsets):
        return pick_rows(
            place, [lefts[o] for o in offsets], [rights[o] for o in offsets],
            groups, per_group, slots, 0, 0, rows,
        )

    near_rows, near_meta = picked(NEAR)
    far_rows, far_meta = picked(FAR)
    far_rows, *own_weights = lax.optimization_barrier(
        (far_rows, gate_weights, up_weights, down_weights)
    )
    weights = [w for own in own_weights for w in (own, swap(own))]
    near_rows = exchange(near_rows)
    near_rows, far_rows = lax.optimization_barrier((near_rows, far_rows))
    far_rows = exchange(far_rows)
    near_line, near_column = slot_keys(place, [near_rows], groups, members, slots, NEAR)
    near_out = expert(place, near_rows, weights, [], [], capacity)
    far_rows, near_out, near_line = lax.optimization_barrier((far_rows, near_out, near_line))
    near_back = exchange(near_out)
    far_line, far_column = slot_keys(place, [far_rows], groups, members, slots, FAR)
    lines = [near_line, far_line]
    lines = lines + [swap(line) for line in lines]
    far_out = expert(place, far_rows, weights, lines, [near_column, far_column], capacity)
    near_back, far_out = lax.optimization_barrier((near_back, far_out))
    far_back = exchange(far_out)
    far_table = score_table(place, far_meta, groups, per_group, slots, blocks)
    near_table = score_table(place, near_meta, groups, per_group, slots, blocks)
    far_parts = combine(far_table, far_back, [far_back], 1, half, blocks, groups)
    near_parts = combine(near_table, far_back, [near_back], 0, half, blocks, groups)
    other, own = (
        scattered(
            dict(zip(FAR + NEAR, far_parts[i : i + blocks] + near_parts[i : i + blocks])), way
        )
        for i, way in ((0, 1), (blocks, -1))
    )
    weight_sum = jnp.maximum(other[:, half : half + 1], 1.0)
    own, other = own / weight_sum, other[:, :half] / weight_sum
    is_first = index % 2 == 0
    left = jnp.where(is_first, own, other)
    right = jnp.where(is_first, other, own)
    return jnp.concatenate([left, right], axis=1).astype(BF16)


def solution(mesh):
    rows = P(("group", "ingroup"), None)
    weights = P(("group", "ingroup"), None, None)
    return jax.shard_map(
        per_device,
        mesh=mesh,
        in_specs=(rows, weights, weights, weights, rows, rows, P(("group", "ingroup"))),
        out_specs=rows,
        check_vma=False,
    )
```

```python
import functools

import jax
import jax.numpy as jnp
from jax import lax
from jax.experimental import pallas as pl
from jax.experimental.pallas import tpu as pltpu
from jax.sharding import PartitionSpec as P

TOPG = 4
META = 128
AT_SCORE, AT_POS, AT_ONE = 8, 16, 17
EMPTY = 1.0e9
NEAR = (0, -1, 1, -2)
FAR = (2, -3, 3, -4)
F32, BF16 = jnp.float32, jnp.bfloat16


def iota(shape, axis):
    return lax.broadcasted_iota(jnp.int32, shape, axis)


def divided(value, by, most):
    total = jnp.zeros_like(value)
    for j in range(1, most):
        total = total + (value >= j * by).astype(jnp.int32)
    return total


def tiles(width, tile):
    return [(at, min(tile, width - at)) for at in range(0, width, tile)]


def call(kernel, name, out_shape, flops, moved, vmem, **more):
    return pl.pallas_call(
        kernel,
        out_shape=out_shape,
        name=name,
        cost_estimate=pl.CostEstimate(flops=flops, bytes_accessed=moved, transcendentals=0),
        compiler_params=pltpu.CompilerParams(vmem_limit_bytes=vmem << 20),
        **more,
    )


WHOLE = pl.BlockSpec(memory_space=pltpu.VMEM)
SCALARS = pl.BlockSpec(memory_space=pltpu.SMEM)


STAYS = pl.BlockSpec(memory_space=pltpu.HBM)


def far_memory(*arrays):
    return [pltpu.with_memory_space_constraint(a, pltpu.HBM) for a in arrays]


def unit(rows):
    return (iota((rows, META), 0) == iota((rows, META), 1)).astype(F32).astype(BF16)


def lines_of(columns, rows):
    return lax.dot_general(
        unit(rows), columns, (((1,), (1,)), ((), ())), preferred_element_type=F32
    )


def start_rows_kernel(rows_ref, ids_ref, scores_ref, pos_ref, left_ref, right_ref):
    half = left_ref.shape[1]
    tok = rows_ref.shape[0]
    lines = [ids_ref[...].astype(F32), scores_ref[...].astype(F32), pos_ref[...].astype(F32)]
    lines.append(jnp.ones((1, tok), F32))
    lines.append(jnp.zeros((14, tok), F32))
    lines = jnp.concatenate(lines, axis=0).astype(BF16)
    meta = lax.dot_general(lines, unit(32), (((0,), (0,)), ((), ())), preferred_element_type=F32)
    left_ref[...] = rows_ref[:, :half]
    right_ref[:, :half] = rows_ref[:, half:]
    right_ref[:, half:] = meta.astype(BF16)


def start_rows(rows, ids, scores, pos):
    tok, model = rows.shape
    half = model // 2
    return call(
        start_rows_kernel,
        "start_rows",
        (jax.ShapeDtypeStruct((tok, half), BF16), jax.ShapeDtypeStruct((tok, half + META), BF16)),
        0,
        4 * tok * model,
        4,
        grid=(1,),
        in_specs=[
            pl.BlockSpec(a.shape, lambda i: (0, 0)) for a in (rows, ids.T, scores.T, pos[None, :])
        ],
        out_specs=(
            pl.BlockSpec((tok, half), lambda i: (0, 0)),
            pl.BlockSpec((tok, half + META), lambda i: (0, 0)),
        ),
    )(*far_memory(rows, ids.T, scores.T, pos[None, :]))


def pick_rows_kernel(place_ref, *refs, groups, per_group, slots, first_block, first_row, rows):
    out_ref, meta_ref, built_ref, sent = refs[-4:]
    count = (len(refs) - 4) // 2
    lefts, rights = refs[:count], refs[count:-4]
    copies = []
    tok, half = lefts[0].shape
    total = tok * count
    meta = jnp.concatenate([b[:, half:] for b in rights], axis=0)
    meta_ref[...] = meta
    meta_t = lines_of(meta, 32)
    expert = (iota((groups, total), 0) * per_group + place_ref[0]).astype(F32)
    hit = jnp.zeros((groups, total), F32)
    for k in range(AT_SCORE):
        hit = hit + (meta_t[k : k + 1, :] == expert).astype(F32)
    first, second = iota((total, total), 0), iota((total, total), 1)
    same = divided(first, tok, count) == divided(second, tok, count)
    before = (same & (first < second)).astype(F32).astype(BF16)
    occurrence = jnp.dot(hit.astype(BF16), before, preferred_element_type=F32)
    block_of = divided(iota((groups, total), 1), tok, count).astype(F32)
    slot = occurrence + slots * (block_of + first_block) - first_row
    slot = jnp.where(hit > 0, slot, -1.0)
    slot = jnp.broadcast_to(slot[:, None, :], (groups, rows, total))
    chosen = (slot == iota((groups, rows, total), 1).astype(F32)).astype(F32)
    chosen = chosen.reshape(groups * rows, total).astype(BF16)
    for start, blocks in ((0, lefts), (half, rights)):
        for at, wide in tiles(blocks[0].shape[1], 512):
            part = jnp.concatenate([b[:, at : at + wide] for b in blocks], axis=0)
            cut = pl.ds(start + at, wide)
            built_ref[:, cut] = jnp.dot(chosen, part, preferred_element_type=F32).astype(BF16)
            copies.append(
                pltpu.make_async_copy(built_ref.at[:, cut], out_ref.at[:, cut], sent.at[len(copies)])
            )
            copies[-1].start()
    for copy in copies:
        copy.wait()


def pick_rows(place, lefts, rights, groups, per_group, slots, first_block, first_row, rows):
    width = lefts[0].shape[1] + rights[0].shape[1]
    total = lefts[0].shape[0] * len(lefts)
    return call(
        functools.partial(
            pick_rows_kernel, groups=groups, per_group=per_group, slots=slots,
            first_block=first_block, first_row=first_row, rows=rows,
        ),
        "pick_rows",
        (pltpu.HBM((groups * rows, width), BF16), jax.ShapeDtypeStruct((total, META), BF16)),
        2 * groups * rows * total * width,
        2 * (groups * rows + total) * width,
        12,
        in_specs=[SCALARS] + [WHOLE] * (2 * len(lefts)),
        out_specs=(STAYS, WHOLE),
        scratch_shapes=[pltpu.VMEM((groups * rows, width), BF16), pltpu.SemaphoreType.DMA((8,))],
    )(place, *lefts, *rights)


def score_table_kernel(place_ref, meta_ref, out_ref, *, groups, per_group, slots, blocks):
    total = meta_ref.shape[0]
    tok = total // blocks
    rows = slots * blocks
    meta = meta_ref[...].astype(F32)
    expert = (iota((total, META), 1) * per_group + place_ref[0]).astype(F32)
    hit = jnp.zeros((total, META), F32)
    score = jnp.zeros((total, META), F32)
    for k in range(AT_SCORE):
        same = (meta[:, k : k + 1] == expert).astype(F32)
        hit = hit + same
        score = score + same * meta[:, AT_SCORE + k : AT_SCORE + k + 1]
    first, second = iota((total, total), 0), iota((total, total), 1)
    same = divided(first, tok, blocks) == divided(second, tok, blocks)
    before = (same & (second < first)).astype(F32).astype(BF16)
    occurrence = jnp.dot(before, hit.astype(BF16), preferred_element_type=F32)
    block_of = divided(iota((total, META), 0), tok, blocks).astype(F32)
    slot = jnp.where(hit > 0, occurrence + slots * block_of, -1.0)
    source, lane = iota((META, groups * rows), 0), iota((META, groups * rows), 1)
    spread = ((lane >= source * rows) & (lane < source * rows + rows)).astype(F32).astype(BF16)
    slot_wide = jnp.dot(slot.astype(BF16), spread, preferred_element_type=F32)
    score_wide = jnp.dot(score.astype(BF16), spread, preferred_element_type=F32)
    column = iota((1, groups * rows), 1)
    column = (column - rows * divided(column, rows, groups)).astype(F32)
    out_ref[...] = jnp.where(slot_wide == column, score_wide, 0.0).astype(BF16)


def score_table(place, meta, groups, per_group, slots, blocks):
    total = meta.shape[0]
    columns = groups * slots * blocks
    return call(
        functools.partial(
            score_table_kernel, groups=groups, per_group=per_group, slots=slots, blocks=blocks
        ),
        "score_table",
        pltpu.HBM((total, columns), BF16),
        2 * total * columns * (2 * META),
        2 * total * columns,
        12,
        grid=(1,),
        in_specs=[SCALARS, pl.BlockSpec((total, META), lambda i: (0, 0))],
        out_specs=pl.BlockSpec((total, columns), lambda i: (0, 0)),
    )(place, meta)


def slot_keys_kernel(place_ref, *refs, groups, members, slots, offsets):
    meta_refs, (line_ref, column_ref) = refs[:-2], refs[-2:]
    z, c = place_ref[0], place_ref[1]
    rows = line_ref.shape[1] // groups
    first = 0
    for meta_ref in meta_refs:
        count = meta_ref.shape[0]
        part = count // groups
        meta = meta_ref[...]
        meta_t = lines_of(meta, 32)

        def key(index, position, valid):
            group = divided(index, part, groups)
            block = divided(index - part * group + first, slots, len(offsets))
            apart = jnp.zeros_like(index)
            for j, offset in enumerate(offsets):
                apart = apart + jnp.where(block == j, offset, 0)
            ring = members // 2
            where = z + apart
            where = jnp.where(where < 0, where + ring, where)
            where = jnp.where(where >= ring, where - ring, where)
            source = (group * members + where * 2 + c).astype(F32)
            return jnp.where(valid > 0, position * (groups * members) + source, EMPTY)

        line = key(iota((1, count), 1), meta_t[AT_POS : AT_POS + 1], meta_t[AT_ONE : AT_ONE + 1])
        at = first * groups
        line_ref[:, at : at + count] = jnp.broadcast_to(line, (line_ref.shape[0], count))
        wide = meta.astype(F32)
        column = key(
            iota((count, 1), 0), wide[:, AT_POS : AT_POS + 1], wide[:, AT_ONE : AT_ONE + 1]
        )
        column = jnp.broadcast_to(column, meta.shape)
        for g in range(groups):
            at = g * rows + first
            column_ref[at : at + part, :] = column[g * part : (g + 1) * part]
        first += part


def slot_keys(place, parts, groups, members, slots, offsets):
    count = sum(rows.shape[0] for rows in parts)
    last = parts[0].shape[1] // META - 1
    return call(
        functools.partial(
            slot_keys_kernel, groups=groups, members=members, slots=slots, offsets=offsets
        ),
        "slot_keys",
        (jax.ShapeDtypeStruct((8, count), F32), jax.ShapeDtypeStruct((count, META), F32)),
        0,
        16 * count * META,
        4,
        grid=(1,),
        in_specs=[SCALARS]
        + [pl.BlockSpec((rows.shape[0], META), lambda i: (0, last)) for rows in parts],
        out_specs=(
            pl.BlockSpec((8, count), lambda i: (0, 0)),
            pl.BlockSpec((count, META), lambda i: (0, 0)),
        ),
    )(place, *parts)


def kept_flags(lines, columns, capacity):
    count = columns[0].shape[0]
    lane = iota((count, META), 1)
    flags = jnp.zeros((count, META), F32)
    for q, column_ref in enumerate(columns):
        own = column_ref[:, :1]
        rank = jnp.zeros(own.shape, F32)
        for line_ref in lines:
            rank = rank + jnp.sum((line_ref[:1, :] < own).astype(F32), axis=1, keepdims=True)
        kept = jnp.where((rank < capacity) & (own < EMPTY), 1.0, 0.0)
        flags = jnp.where(lane == q, kept, flags)
    return flags.astype(BF16)


def expert_kernel(
    place_ref, gate_own, gate_other, up_own, up_other, down_own, down_other, *refs, lines, capacity
):
    line_refs, refs = refs[:lines], refs[lines:]
    column_refs, refs = refs[: lines // 2], refs[lines // 2 :]
    came_ref, out_ref, total_ref, rows_ref, came = refs
    half = gate_own.shape[1]
    c = place_ref[1]
    step = pl.program_id(0)

    @pl.when(step == 0)
    def _():
        copy = pltpu.make_async_copy(came_ref, rows_ref, came)
        copy.start()
        if lines:
            out_ref[:, 2 * half :] = kept_flags(line_refs, column_refs, capacity)
        copy.wait()

    own = rows_ref[:, pl.ds(pl.multiple_of(c * half, 128), half)]
    other = rows_ref[:, pl.ds(pl.multiple_of((1 - c) * half, 128), half)]
    gate = jnp.dot(own, gate_own[0], preferred_element_type=F32) + jnp.dot(
        other, gate_other[0], preferred_element_type=F32
    )
    up = jnp.dot(own, up_own[0], preferred_element_type=F32) + jnp.dot(
        other, up_other[0], preferred_element_type=F32
    )
    hidden = (gate / (1.0 + jnp.exp(-gate)) * up).astype(BF16)
    for at, down in ((0, down_own), (half, down_other)):
        part = jnp.dot(hidden, down[0], preferred_element_type=F32)
        cut = slice(at, at + half)

        @pl.when(step == 0)
        def _():
            total_ref[:, cut] = part

        @pl.when((step > 0) & (step < pl.num_programs(0) - 1))
        def _():
            total_ref[:, cut] = total_ref[:, cut] + part

        @pl.when(step == pl.num_programs(0) - 1)
        def _():
            out_ref[:, cut] = (total_ref[:, cut] + part).astype(BF16)


def expert(place, rows, weights, lines, columns, capacity):
    count, width = rows.shape
    half, units = weights[0].shape[1:]
    tile = 256
    weight = pl.BlockSpec((1, half, tile), lambda i: (0, 0, i))
    down = pl.BlockSpec((1, tile, half), lambda i: (0, i, 0))
    out = 2 * half + (META if lines else 0)
    return call(
        functools.partial(expert_kernel, lines=len(lines), capacity=capacity),
        "expert",
        pltpu.HBM((count, out), BF16),
        12 * count * half * units,
        2 * (count * width + 6 * half * units + count * out),
        44,
        grid=(units // tile,),
        in_specs=[SCALARS]
        + [weight] * 4
        + [down] * 2
        + [pl.BlockSpec((8, count), lambda i: (0, 0))] * len(lines)
        + [pl.BlockSpec((count, META), lambda i: (0, 0))] * len(columns)
        + [STAYS],
        out_specs=pl.BlockSpec((count, out), lambda i: (0, 0)),
        scratch_shapes=[
            pltpu.VMEM((count, 2 * half), F32),
            pltpu.VMEM((count, width), BF16),
            pltpu.SemaphoreType.DMA,
        ],
    )(place, *far_memory(*weights), *lines, *columns, *far_memory(rows))


def combine_kernel(table_ref, flag_ref, *refs, parts, pieces, groups, flag):
    part_refs, out_refs = refs[:parts], refs[parts : -parts - 2]
    kept_refs, built_ref, sent = refs[-parts - 2 : -2], refs[-2], refs[-1]
    tok = out_refs[0].shape[0]
    blocks = len(out_refs) // pieces
    step, steps = pl.program_id(0), pl.num_programs(0)
    half = out_refs[-1].shape[1]
    tile = 2 * half // steps
    at = pl.ds(pl.multiple_of(step * tile, 128), tile)

    @pl.when(step == 0)
    def _():
        table = table_ref[...].astype(F32) * lines_of(flag_ref[...], 8)[flag : flag + 1]
        total = jnp.sum(table, axis=1, keepdims=True)
        built_ref[:, 2 * half :] = jnp.broadcast_to(total, (blocks * tok, META)).astype(BF16)
        table = table.astype(BF16)
        columns = table.shape[1]
        first = 0
        for kept_ref in kept_refs:
            count = kept_ref.shape[1]
            part = count // groups
            if count == columns:
                kept_ref[...] = table
            else:
                source, lane = iota((columns, count), 0), iota((columns, count), 1)
                group = divided(lane, part, groups)
                taken = source == (columns // groups - part) * group + lane + first
                taken = taken.astype(F32).astype(BF16)
                kept_ref[...] = jnp.dot(table, taken, preferred_element_type=F32).astype(BF16)
            first += part

    total = None
    for kept_ref, part_ref in zip(kept_refs, part_refs):
        rows = part_ref[...] if part_ref.shape[1] == tile else part_ref[:, at]
        product = jnp.dot(kept_ref[...], rows, preferred_element_type=F32)
        total = product if total is None else total + product
    built_ref[:, at] = total.astype(BF16)

    def copies(p):
        made = []
        for b in range(blocks):
            to = out_refs[p * blocks + b]
            source = built_ref.at[pl.ds(b * tok, tok), pl.ds((pieces - 1 - p) * half, to.shape[1])]
            made.append(pltpu.make_async_copy(source, to, sent.at[p, b]))
        return made

    for p in range(pieces):

        @pl.when(step == (pieces - p) * steps // pieces - 1)
        def _():
            for copy in copies(p):
                copy.start()

    @pl.when(step == steps - 1)
    def _():
        for p in range(pieces):
            for copy in copies(p):
                copy.wait()


def combine(table, far, parts, flag, half, blocks, groups):
    total, count = table.shape
    tok = total // blocks
    tile = half
    last = far.shape[1] // META - 1
    return call(
        functools.partial(combine_kernel, parts=len(parts), pieces=2, groups=groups, flag=flag),
        "combine",
        (pltpu.HBM((tok, half + META), BF16),) * blocks + (pltpu.HBM((tok, half), BF16),) * blocks,
        4 * total * count * half,
        4 * (total * count + (count + total) * half),
        16,
        grid=(2 * half // tile,),
        in_specs=[
            pl.BlockSpec((total, count), lambda i: (0, 0)),
            pl.BlockSpec((count, META), lambda i: (0, last)),
        ]
        + [
            WHOLE if rows is far else pl.BlockSpec((rows.shape[0], tile), lambda i: (0, i))
            for rows in parts
        ],
        out_specs=(STAYS,) * (2 * blocks),
        scratch_shapes=[pltpu.VMEM((total, rows.shape[0]), BF16) for rows in parts]
        + [
            pltpu.VMEM((total, 2 * half + META), BF16),
            pltpu.SemaphoreType.DMA((2, blocks)),
        ],
    )(*far_memory(table), far, *parts)


def per_device(
    activations, gate_weights, up_weights, down_weights, expert_ids, gate_scores, arrival_pos
):
    groups = lax.axis_size("group")
    members = lax.axis_size("ingroup")
    per_group = ring = members // 2
    tok = activations.shape[0]
    half = activations.shape[1] // 2
    top_picks = expert_ids.shape[1]
    capacity = 2 * top_picks * tok
    group_most = min(tok, 3 * tok * TOPG // (2 * groups))
    slots = (2 * group_most + per_group - 1) // per_group
    index = lax.axis_index("ingroup")
    place = jnp.stack([index // 2, index % 2]).astype(jnp.int32)
    partner = [(i, i ^ 1) for i in range(members)]

    def along(shard, by):
        hop = [(i, (i // 2 + by) % ring * 2 + i % 2) for i in range(members)]
        return lax.ppermute(shard, "ingroup", hop)

    def swap(shard):
        return lax.ppermute(shard, "ingroup", partner)

    def exchange(rows):
        return lax.all_to_all(rows, "group", split_axis=0, concat_axis=0, tiled=True)

    def gathered(shard, way):
        held = {0: shard}
        for step in range(1, ring // 2):
            held[-step] = along(held[1 - step], 1)
            held[step] = along(held[step - 1], -1)
        held[-ring // 2] = along(held[way * (ring // 2 - 1)], -way)
        return held

    def added(moving, part):
        return (moving.astype(F32) + part.astype(F32)).astype(BF16)

    def scattered(parts, way):
        sums = parts[0].astype(F32)
        for side in (way, -way):
            steps = [side * step for step in range(ring // 2 - 1, 0, -1)]
            moving = parts[-ring // 2] if side == way else parts[steps.pop(0)]
            for step in steps:
                moving = added(along(moving, side), parts[step])
            sums = sums + along(moving, side).astype(F32)
        return sums

    left, right = start_rows(activations, expert_ids, gate_scores, arrival_pos)
    lefts, rights = gathered(left, -1), gathered(right, 1)
    rows = slots * len(NEAR)
    blocks = len(NEAR)

    def picked(offsets):
        return pick_rows(
            place, [lefts[o] for o in offsets], [rights[o] for o in offsets],
            groups, per_group, slots, 0, 0, rows,
        )

    near_rows, near_meta = picked(NEAR)
    far_rows, far_meta = picked(FAR)
    far_rows, *own_weights = lax.optimization_barrier(
        (far_rows, gate_weights, up_weights, down_weights)
    )
    weights = [w for own in own_weights for w in (own, swap(own))]
    near_rows = exchange(near_rows)
    near_rows, far_rows = lax.optimization_barrier((near_rows, far_rows))
    far_rows = exchange(far_rows)
    near_line, near_column = slot_keys(place, [near_rows], groups, members, slots, NEAR)
    near_out = expert(place, near_rows, weights, [], [], capacity)
    far_rows, near_out, near_line = lax.optimization_barrier((far_rows, near_out, near_line))
    near_back = exchange(near_out)
    far_line, far_column = slot_keys(place, [far_rows], groups, members, slots, FAR)
    lines = [near_line, far_line]
    lines = lines + [swap(line) for line in lines]
    far_out = expert(place, far_rows, weights, lines, [near_column, far_column], capacity)
    far_table = score_table(place, far_meta, groups, per_group, slots, blocks)
    near_table = score_table(place, near_meta, groups, per_group, slots, blocks)
    near_back, far_out, far_table, near_table = lax.optimization_barrier(
        (near_back, far_out, far_table, near_table)
    )
    far_back = exchange(far_out)
    far_parts = combine(far_table, far_back, [far_back], 1, half, blocks, groups)
    near_parts = combine(near_table, far_back, [near_back], 0, half, blocks, groups)
    other, own = (
        scattered(
            dict(zip(FAR + NEAR, far_parts[i : i + blocks] + near_parts[i : i + blocks])), way
        )
        for i, way in ((0, 1), (blocks, -1))
    )
    weight_sum = jnp.maximum(other[:, half : half + 1], 1.0)
    own, other = own / weight_sum, other[:, :half] / weight_sum
    is_first = index % 2 == 0
    left = jnp.where(is_first, own, other)
    right = jnp.where(is_first, other, own)
    return jnp.concatenate([left, right], axis=1).astype(BF16)


def solution(mesh):
    rows = P(("group", "ingroup"), None)
    weights = P(("group", "ingroup"), None, None)
    return jax.shard_map(
        per_device,
        mesh=mesh,
        in_specs=(rows, weights, weights, weights, rows, rows, P(("group", "ingroup"))),
        out_specs=rows,
        check_vma=False,
    )
```
